32 devices in a mesh: bt: 16 (over z, x, core), ch: 2 (over y).
Axes of the slice: x: 2, y: 2, z: 4, core: 2. Of those that a mesh axis runs over, the one named last changes fastest.
Arguments:
- visibility: float32 [2, 4, 64, 4096], P(None, None, 'ch', 'bt'), may hold values from -6 to 6
- cell_offset: float32 [2, 4, 64, 4096], P(None, None, 'ch', 'bt'), may hold values from 2 to 30
- station_gain: float32 [2, 64, 512], P(None, 'ch'), may hold values from 0.1 to 1.9
- stations: int32 [4096, 2], P('bt'), may hold values from 0 to 511, all different within a row
- row_band: int32 [4096, 1], replicated, may hold values from 0 to 15; in each aligned block of 128 rows (0 to 127, 128 to 255, ...) at most 16 rows name the same one
- tile_offset: int32 [4096], replicated, may hold values from 0 to 2047
Outputs:
- sky_image: float32 [2, 8192, 8192], P(None, ('bt', 'ch'))
The draws below stay inside these ranges and needn't reach their ends.
Inputs may be any that keep to these rules, and one draw needn't show every extreme that they name: `row_band`: in each aligned run of 128 blocks (one bt index's blocks of one column band) no row band is named by more than 16 blocks. The two stations of a block differ.
All inputs are finite; a program needn't handle non-finite values.
Results may differ from the reference program's by a relative error of at most 0.0003.
Values sent between devices are 32-bit elements; how exact they have to be, the bound alone decides.
No kernel may reach another device: no remote copies, remote signals or barrier semaphores. Data moves between devices by JAX's collectives and lax.ppermute only.
A program may use at most 192 MiB of HBM per device.

```python
import math
import jax
import jax.numpy as jnp
import numpy as np
from jax import lax

SUB = 32
TSLOT = 4
CHANNELS = 64
STATIONS = 512
NB = 256
BLOCKS = 4096
NBC = 128
G = 8192
GT = 256
TRB = 16
TCB = 128
CAPR = 16
N_BT = 16


def place_ends(entries, rng, smallest, high):
    index_at = [jax.random.randint(jax.random.fold_in(rng, axis), (), 0, length) for axis, length in enumerate(entries.shape)]
    widest = entries.shape.index(max(entries.shape))
    neighbour = index_at[:widest] + [(index_at[widest] + 1) % entries.shape[widest]] + index_at[widest + 1:]
    return entries.at[tuple(index_at)].set(smallest).at[tuple(neighbour)].set(high)


def levels(rng, extent, cuts, least, largest):
    def one(axis_at, blocks):
        draws = jax.random.uniform(jax.random.fold_in(jax.random.fold_in(rng, 6), axis_at), (blocks,), jnp.float32, least / len(cuts), largest / len(cuts))
        return jnp.repeat(jnp.exp(draws), extent[axis_at] // blocks).reshape((-1,) + (1,) * (len(extent) - axis_at - 1))

    factor_of = one(*cuts[0])
    for cut in cuts[1:]:
        factor_of = factor_of * one(*cut)
    return factor_of


def different_ones(rng, rows, amount, top, lift):
    ranking = jax.random.permutation(jax.random.fold_in(rng, 1), amount)
    favour = ranking
    for power in range(3):
        favour = favour * favour // amount
    favour = favour * lift // amount
    chance = jax.random.randint(jax.random.fold_in(rng, 2), (rows, amount), 0, 4096) + favour
    holders = jax.random.permutation(jax.random.fold_in(rng, 3), rows)[jnp.arange(amount) % rows]
    chance = jnp.where(jnp.arange(rows)[:, None] == holders[None, :], 1 << 14, chance)
    merit = chance * amount + jnp.arange(amount)
    return lax.top_k(merit.astype(jnp.int32), top)[1].astype(jnp.int32)


def shared_out(own_key, own, number, rows, amount, top, reach, slope):
    ranking = jax.random.permutation(own_key, amount)
    heavy_load, common = shares(amount, rows * top, reach, slope, True), shares(amount, rows * top, reach, slope, False)
    places = jnp.arange(amount)

    def named(lengths, turn):
        used = int((lengths > 0).sum())
        fixed = max(1, used // 4)
        moved = fixed + (places - fixed + turn * (used - fixed)) % max(1, amount - fixed)
        return jnp.zeros((amount,), jnp.int32).at[ranking[jnp.where(places < fixed, places, moved)]].set(jnp.asarray(lengths, jnp.int32))

    lengths = jnp.where(number % 4 == 0, named(heavy_load, number // 4), named(common, number - number // 4 - 1))
    mixed = jax.random.permutation(jax.random.fold_in(own, 3), amount)
    giver, taker = mixed[0:amount // 2 * 2:2], mixed[1:amount // 2 * 2:2]
    slack = jnp.minimum(lengths[giver] - 1, reach - lengths[taker]) // 2
    slack = jnp.where((giver == ranking[0]) | (taker == ranking[0]) | (lengths[taker] == 0), 0, jnp.maximum(slack, 0))
    moved = jax.random.randint(jax.random.fold_in(own, 4), (amount // 2,), 0, 1 << 20) % (slack + 1)
    lengths = lengths.at[giver].add(-moved).at[taker].add(moved)
    members = jnp.searchsorted(jnp.cumsum(lengths), jnp.arange(rows * top), side="right").astype(jnp.int32)
    table = members.reshape(top, rows).T
    table = table[jax.random.permutation(jax.random.fold_in(own, 1), rows)]
    turn = jax.random.randint(jax.random.fold_in(own, 2), (rows, 1), 0, top)
    return jnp.take_along_axis(table, (jnp.arange(top)[None, :] + turn) % top, axis=1)


def shares(number_of, total, reach, lean, full):
    portions = [(1 << 20) // math.isqrt(standing ** lean) + 1 for standing in range(1, number_of + 1)]
    largest = reach if full else min(reach, max(-(-total // number_of), total * portions[0] // sum(portions)))
    least = 1 if total - largest >= number_of - 1 else 0
    counts, spare = [largest] + [least] * (number_of - 1), total - largest - least * (number_of - 1)
    while spare > 0:
        movable = [i for i in range(1, number_of) if counts[i] < largest] or [i for i in range(1, number_of) if counts[i] < reach]
        mass, left = sum([portions[i] for i in movable]), spare
        for i in movable:
            extra = min(reach - counts[i], max(1, left * portions[i] // mass), spare)
            counts[i] = counts[i] + extra
            spare = spare - extra
    return np.array(counts)


def normal_values(stream_key, shape, width, reach, shards=(), held_as=jnp.bfloat16):
    factor_of = levels(stream_key, shape, shards, -0.22, 0.18) if shards else 1.0
    drawn = jax.random.normal(stream_key, shape, jnp.float32) * width * factor_of
    return jnp.minimum(jnp.maximum(drawn, -reach), reach).astype(held_as)


def setup_inputs(seed: int = 0) -> dict:
    arg_keys = jax.random.split(jax.random.key(seed), 7)
    visibility = normal_values(arg_keys[0], (2, TSLOT, CHANNELS, BLOCKS), 1.0, 6.0, ((2, 2), (3, 16)), jnp.float32)
    cell_offset = jnp.clip(2.0 + 28.0 * jax.random.uniform(arg_keys[1], (2, TSLOT, CHANNELS, BLOCKS), jnp.float32) ** levels(arg_keys[1], (2, TSLOT, CHANNELS, BLOCKS), ((2, 2), (3, 16)), -0.2, 0.2), 2.0, 30.0)
    station_gain = jnp.clip(1.0 + 0.18 * jax.random.normal(arg_keys[2], (2, CHANNELS, STATIONS), jnp.float32), 0.1, 1.9)
    stations = different_ones(arg_keys[3], BLOCKS, STATIONS, 2, 0)
    row_band_keys = jax.random.split(jax.random.fold_in(arg_keys[4], 1), BLOCKS // NBC)
    row_band_turns = jax.random.permutation(jax.random.fold_in(arg_keys[4], 3), BLOCKS // NBC)
    row_band = jax.vmap(lambda own, number: shared_out(jax.random.fold_in(arg_keys[4], 2), own, number, NBC, N_BT, 1, CAPR, 2))(row_band_keys, row_band_turns).reshape((BLOCKS, 1))
    tile_offset = place_ends(jax.random.randint(arg_keys[5], (BLOCKS,), 0, TRB * TCB), jax.random.fold_in(arg_keys[5], 1), 0, (TRB * TCB) - 1).astype(jnp.int32)
    return {"visibility": visibility, "cell_offset": cell_offset, "station_gain": station_gain, "stations": stations, "row_band": row_band, "tile_offset": tile_offset}


highest = lax.Precision.HIGHEST
full_turn = 2.0 * math.pi

def complex_einsum(form, left_side, right_side):
    real_part = jnp.einsum(form, left_side[0], right_side[0], precision=highest) - jnp.einsum(form, left_side[1], right_side[1], precision=highest)
    imag_part = jnp.einsum(form, left_side[0], right_side[1], precision=highest) + jnp.einsum(form, left_side[1], right_side[0], precision=highest)
    return jnp.stack([real_part, imag_part])

def centred_offsets(length):
    return (jnp.arange(length, dtype=jnp.float32) - length // 2) / length

def phasor_pair(coords, length):
    angles = (full_turn * centred_offsets(length))[None, :, None] * coords[:, None, :]
    return jnp.stack([jnp.cos(angles), jnp.sin(angles)])

def tile_table(length):
    positions = jnp.arange(length, dtype=jnp.int32)
    product = positions[:, None] * (positions[None, :] - length // 2) % length
    angles = -full_turn * product.astype(jnp.float32) / length
    centred = centred_offsets(length)
    tapers = jnp.exp(-4.0 * centred * centred) / math.sqrt(length)
    return jnp.stack([jnp.cos(angles) * tapers[None, :], jnp.sin(angles) * tapers[None, :]])

def weighted_vis(visibility, gain_first, gain_second):
    product_real = gain_first[0] * gain_second[0] + gain_first[1] * gain_second[1]
    product_imag = gain_first[1] * gain_second[0] - gain_first[0] * gain_second[1]
    real_part = visibility[0] * product_real[None] - visibility[1] * product_imag[None]
    imag_part = visibility[0] * product_imag[None] + visibility[1] * product_real[None]
    return jnp.stack([real_part, imag_part])

def image_subgrids(weighted, coords):
    phase_first = phasor_pair(coords[0], SUB)
    phase_second = phasor_pair(coords[1], SUB)
    scaled = jnp.stack([weighted[0][:, None, :] * phase_first[0] - weighted[1][:, None, :] * phase_first[1], weighted[0][:, None, :] * phase_first[1] + weighted[1][:, None, :] * phase_first[0]])
    return complex_einsum('klb,kmb->lmb', scaled, phase_second)

def to_tiles(subgrid_image):
    factor_table = tile_table(SUB)
    partial_value = complex_einsum('pl,lmb->pmb', factor_table, subgrid_image)
    return complex_einsum('qm,pmb->pqb', factor_table, partial_value)

def reference(visibility, cell_offset, station_gain, stations, row_band, tile_offset):
    gain_first = station_gain[:, :, stations[:, 0]]
    gain_second = station_gain[:, :, stations[:, 1]]
    weighted = weighted_vis(visibility, gain_first, gain_second)
    grouped_weights = weighted.reshape(2, TSLOT * CHANNELS, N_BT, NB).transpose(2, 0, 1, 3)
    grouped_coords = cell_offset.reshape(2, TSLOT * CHANNELS, N_BT, NB).transpose(2, 0, 1, 3)

    def one_group(packed):
        return to_tiles(image_subgrids(packed[0], packed[1]))
    tile_stack = lax.map(one_group, (grouped_weights, grouped_coords))
    tile_stack = tile_stack.transpose(0, 4, 1, 2, 3).reshape(BLOCKS, 2, SUB, SUB)
    block_index = jnp.arange(BLOCKS, dtype=jnp.int32)
    tile_row = row_band[:, 0] * TRB + tile_offset // TCB
    tile_column = block_index % NB // NBC * TCB + tile_offset % TCB
    grid_cells = jnp.zeros((GT, GT, 2, SUB, SUB), jnp.float32).at[tile_row, tile_column].add(tile_stack)
    grid_cells = grid_cells.transpose(2, 0, 3, 1, 4).reshape(2, G, G)
    complex_grid = lax.complex(grid_cells[0], grid_cells[1])
    sky_values = jnp.fft.ifft2(complex_grid) * (G / math.sqrt(TSLOT * CHANNELS))
    return jnp.stack([jnp.real(sky_values), jnp.imag(sky_values)]).astype(jnp.float32)
```

```python
import functools
import math

import jax
import jax.numpy as jnp
import numpy as np
from jax import lax
from jax.experimental import pallas as pl
from jax.experimental.pallas import tpu as pltpu
from jax.sharding import PartitionSpec as P

SUB = 32
G1 = 64
G2 = 128
TSLOT = 4
CHANNELS = 64


highest = lax.Precision.HIGHEST
full_turn = 2.0 * math.pi


def complex_einsum(form, left_side, right_side):
    real_part = jnp.einsum(form, left_side[0], right_side[0], precision=highest) - jnp.einsum(
        form, left_side[1], right_side[1], precision=highest
    )
    imag_part = jnp.einsum(form, left_side[0], right_side[1], precision=highest) + jnp.einsum(
        form, left_side[1], right_side[0], precision=highest
    )
    return jnp.stack([real_part, imag_part])


def complex_product(left_side, right_side):
    return jnp.stack(
        [
            left_side[0] * right_side[0] - left_side[1] * right_side[1],
            left_side[0] * right_side[1] + left_side[1] * right_side[0],
        ]
    )


def centred_offsets(length):
    return (jnp.arange(length, dtype=jnp.float32) - length // 2) / length


def phasor_pair(coords, length):
    angles = (full_turn * centred_offsets(length))[None, :, None] * coords[:, None, :]
    return jnp.stack([jnp.cos(angles), jnp.sin(angles)])


def tile_table(length):
    positions = jnp.arange(length, dtype=jnp.int32)
    product = positions[:, None] * (positions[None, :] - length // 2) % length
    angles = -full_turn * product.astype(jnp.float32) / length
    centred = centred_offsets(length)
    tapers = jnp.exp(-4.0 * centred * centred) / math.sqrt(length)
    return jnp.stack([jnp.cos(angles) * tapers[None, :], jnp.sin(angles) * tapers[None, :]])


def weighted_vis(visibility, gain_first, gain_second):
    product_real = gain_first[0] * gain_second[0] + gain_first[1] * gain_second[1]
    product_imag = gain_first[1] * gain_second[0] - gain_first[0] * gain_second[1]
    real_part = visibility[0] * product_real[None] - visibility[1] * product_imag[None]
    imag_part = visibility[0] * product_imag[None] + visibility[1] * product_real[None]
    return jnp.stack([real_part, imag_part])


def image_subgrids(weighted, coords):
    phase_first = phasor_pair(coords[0], SUB)
    phase_second = phasor_pair(coords[1], SUB)
    scaled = jnp.stack(
        [
            weighted[0][:, None, :] * phase_first[0] - weighted[1][:, None, :] * phase_first[1],
            weighted[0][:, None, :] * phase_first[1] + weighted[1][:, None, :] * phase_first[0],
        ]
    )
    return complex_einsum("klb,kmb->lmb", scaled, phase_second)


def to_tiles(subgrid_image):
    factor_table = tile_table(SUB)
    partial_value = complex_einsum("pl,lmb->pmb", factor_table, subgrid_image)
    return complex_einsum("qm,pmb->pqb", factor_table, partial_value)


def dft_table(length):
    positions = jnp.arange(length, dtype=jnp.int32)
    angles = (
        full_turn * (positions[:, None] * positions[None, :] % length).astype(jnp.float32) / length
    )
    return jnp.stack([jnp.cos(angles), jnp.sin(angles)])


def twiddle_table(outer_length, inner_length):
    full_length = outer_length * inner_length
    outer_index = jnp.arange(outer_length, dtype=jnp.int32)
    inner_index = jnp.arange(inner_length, dtype=jnp.int32)
    angles = (
        full_turn
        * (outer_index[:, None] * inner_index[None, :] % full_length).astype(jnp.float32)
        / full_length
    )
    return jnp.stack([jnp.cos(angles), jnp.sin(angles)])


def transform_rows(cells):
    columns = cells.shape[2]
    blocked = cells.reshape(2, G1, G2, columns)
    section_one = complex_einsum("kn,nmc->kmc", dft_table(G1), blocked)
    section_one = complex_product(section_one, twiddle_table(G1, G2)[:, :, :, None])
    section_two = complex_einsum("mn,knc->mkc", dft_table(G2), section_one)
    return section_two.reshape(2, G1 * G2, columns)


def transform_columns(cells):
    row_count = cells.shape[1]
    blocked = cells.reshape(2, row_count, G1, G2)
    section_one = complex_einsum("kn,rnm->rkm", dft_table(G1), blocked)
    section_one = complex_product(section_one, twiddle_table(G1, G2)[:, None, :, :])
    section_two = complex_einsum("mn,rkn->rmk", dft_table(G2), section_one)
    return section_two.reshape(2, row_count, G1 * G2)


def band_ranks(bands, band_count):
    marked = (bands[:, :, None] == jnp.arange(band_count, dtype=jnp.int32)[None, None, :]).astype(
        jnp.int32
    )
    before = jnp.cumsum(marked, axis=1) - marked
    return jnp.sum(before * marked, axis=2)


def station_pick(chosen, station_count):
    return (jnp.arange(station_count, dtype=jnp.int32)[:, None] == chosen[None, :]).astype(
        jnp.float32
    )


def shards(visibility, cell_offset, station_gain, stations, row_band, tile_offset):
    bt_count = lax.axis_size("bt")
    ch_count = lax.axis_size("ch")
    bt_position = lax.axis_index("bt")
    ch_position = lax.axis_index("ch")
    blocks = visibility.shape[3]
    per_band = blocks // ch_count
    tiles_across = G1 * G2 // SUB
    rows_band = tiles_across // bt_count
    cols_band = tiles_across // ch_count
    capacity = max(2, 2 * blocks // (ch_count * bt_count))
    slot_count = bt_count * capacity
    station_count = station_gain.shape[2]
    gain_first = jnp.einsum(
        "xcs,sb->xcb", station_gain, station_pick(stations[:, 0], station_count), precision=highest
    )
    gain_second = jnp.einsum(
        "xcs,sb->xcb", station_gain, station_pick(stations[:, 1], station_count), precision=highest
    )
    weighted_full = weighted_vis(visibility, gain_first, gain_second)
    band_weights, band_coords = (
        lax.all_to_all(weighted_full, "ch", split_axis=3, concat_axis=2, tiled=True),
        lax.all_to_all(cell_offset, "ch", split_axis=3, concat_axis=2, tiled=True),
    )
    tile_stack = to_tiles(
        image_subgrids(band_weights.reshape(2, -1, per_band), band_coords.reshape(2, -1, per_band))
    )
    band_table = row_band.reshape(bt_count, blocks)
    band_part = lax.dynamic_slice_in_dim(band_table, ch_position * per_band, per_band, 1)
    rank_part = band_ranks(band_part, bt_count)
    own_band = lax.dynamic_index_in_dim(band_part, bt_position, 0, keepdims=False)
    own_rank = lax.dynamic_index_in_dim(rank_part, bt_position, 0, keepdims=False)
    own_slot = own_band * capacity + own_rank
    slot_range = jnp.arange(slot_count, dtype=jnp.int32)
    chooser = (own_slot[:, None] == slot_range[None, :]).astype(jnp.float32)
    outbound = jnp.einsum("xpqw,ws->xpqs", tile_stack, chooser, precision=highest)
    inbound = lax.all_to_all(outbound, "bt", split_axis=3, concat_axis=3, tiled=True)
    landed = band_part == bt_position
    slot_index = jnp.arange(bt_count, dtype=jnp.int32)[:, None] * capacity + rank_part
    slot_hits = ((slot_index[:, :, None] == slot_range[None, None, :]) & landed[:, :, None]).astype(
        jnp.float32
    )
    offset_table = tile_offset.reshape(bt_count, blocks)
    offset_part = lax.dynamic_slice_in_dim(offset_table, ch_position * per_band, per_band, 1)
    tile_range = jnp.arange(rows_band * cols_band, dtype=jnp.int32)
    tile_hits = (offset_part[:, :, None] == tile_range[None, None, :]).astype(jnp.float32)
    placing = jnp.einsum("iws,iwt->st", slot_hits, tile_hits, precision=highest)
    placed = jnp.einsum("xpqs,st->xpqt", inbound, placing, precision=highest)
    grid_block = placed.reshape(2, SUB, SUB, rows_band, cols_band).transpose(0, 3, 1, 4, 2)
    grid_block = grid_block.reshape(2, rows_band * SUB, cols_band * SUB)
    row_span = grid_block.shape[1]
    narrow = grid_block.shape[2] // bt_count
    sending = (
        grid_block.reshape(2, row_span, bt_count, narrow)
        .transpose(0, 2, 1, 3)
        .reshape(2, bt_count, row_span * narrow)
    )
    gathered = lax.all_to_all(sending, "bt", split_axis=1, concat_axis=1, tiled=True)
    along_rows = transform_rows(gathered.reshape(2, bt_count * row_span, narrow))
    spread = lax.all_to_all(
        lax.all_to_all(along_rows, "bt", split_axis=1, concat_axis=2, tiled=True),
        "ch",
        split_axis=1,
        concat_axis=2,
        tiled=True,
    )
    scale = 1.0 / (G1 * G2 * math.sqrt(TSLOT * CHANNELS))
    return transform_columns(spread) * scale

ROWS = 256
CHUNKS = 4
CELLS = 8
SLOT = 32
MIB = 1024 * 1024
f32 = jnp.float32
bf16 = jnp.bfloat16


def split_table(table):
    table = np.asarray(table, np.float64)
    high = table.astype(np.float32).astype(bf16)
    low = (table - high.astype(np.float64)).astype(np.float32).astype(bf16)
    return high, low


def real_form(table):
    return np.block([[table.real, table.imag], [-table.imag, table.real]])


def tile_matrix():
    index = np.arange(SUB)
    centred = (index - SUB // 2) / SUB
    taper = np.exp(-4.0 * centred * centred) / math.sqrt(SUB)
    return np.exp(-2j * math.pi * index[:, None] * centred[None, :]) * taper[None, :]


def cell_order():
    return [8 * coarse + fine for fine in range(8) for coarse in range(4)]


def chunk_rows():
    return [(chunk * CELLS, (chunk + 1) * CELLS) for chunk in range(CHUNKS)]


def subgrid_side_table():
    ordered = tile_matrix()[cell_order()]
    sides = real_form(ordered.T).T.reshape(2, SUB, 2 * SUB)
    rows = [sides[:, start:end].reshape(-1, 2 * SUB) for start, end in chunk_rows()]
    high, low = split_table(np.concatenate(rows, axis=0))
    return np.concatenate([high, high, low, low], axis=1)


def row_tables(devices):
    length = G1 * G2
    rows = np.arange(length)
    turn = (rows[:, None] * np.arange(SUB)[None, :]) % length
    full = np.exp(2j * math.pi * turn / length) @ tile_matrix()
    tables = []
    for device in range(devices):
        part = full[device * ROWS : (device + 1) * ROWS].T
        high, low = split_table(real_form(part))
        tables.append(np.concatenate([high, high, low, low], axis=0))
    return np.stack(tables)


def tile_row_phases():
    angle = 2 * math.pi * (np.outer(np.arange(256), np.arange(ROWS)) % 256) / 256
    return np.concatenate([np.cos(angle), np.sin(angle)], axis=1).astype(np.float32)


def tile_column_tables(first_column):
    scale = 1.0 / (G1 * G2 * math.sqrt(TSLOT * CHANNELS))
    index = np.arange(256)
    turn = np.outer((index + first_column) % 256, index) % 256
    high, low = split_table(real_form(np.exp(2j * math.pi * turn / 256) * scale))
    return np.stack([high, low])


def coarse_twiddles():
    angle = 2 * math.pi * np.outer(np.arange(4), np.arange(256)) / 1024
    return np.stack([np.cos(angle), np.sin(angle)], axis=1).astype(np.float32)


def fine_twiddles():
    turn = np.arange(4)[:, None] * 256 + np.arange(256)[None, :]
    angle = 2 * math.pi * np.arange(8)[:, None, None] * turn[None] / (G1 * G2)
    return np.stack([np.cos(angle), np.sin(angle)], axis=2).astype(np.float32)


def split_value(value):
    high = value.astype(bf16)
    low = (value - high.astype(f32)).astype(bf16)
    return high, low


def cmul(left, right):
    return (
        left[0] * right[0] - left[1] * right[1],
        left[0] * right[1] + left[1] * right[0],
    )


def weigh_kernel(position_ref, vis_ref, off_ref, gain_ref, station_ref, own_ref, other_ref):
    station_count = gain_ref.shape[1]
    blocks = station_ref.shape[1]
    channels = vis_ref.shape[2]
    numbers = lax.broadcasted_iota(jnp.int32, (station_count, blocks), 0)
    gains = gain_ref[...]

    def pick(which):
        chosen = (numbers == station_ref[which : which + 1, :]).astype(f32)
        return jnp.dot(gains, chosen, precision=highest, preferred_element_type=f32)

    first, second = pick(0), pick(1)
    first_re, first_im = first[:channels], first[channels:]
    second_re, second_im = second[:channels], second[channels:]
    gain = (
        first_re * second_re + first_im * second_im,
        first_im * second_re - first_re * second_im,
    )
    weighted = [cmul((vis_ref[0, t], vis_ref[1, t]), gain) for t in range(TSLOT)]
    planes = [
        jnp.concatenate([w[0] for w in weighted], axis=0),
        jnp.concatenate([w[1] for w in weighted], axis=0),
        jnp.concatenate([off_ref[0, t] for t in range(TSLOT)], axis=0),
        jnp.concatenate([off_ref[1, t] for t in range(TSLOT)], axis=0),
    ]
    half = blocks // 2
    first_side = position_ref[0] == 0
    for number, plane in enumerate(planes):
        turned = plane.T
        own_ref[number] = jnp.where(first_side, turned[:half], turned[half:])
        other_ref[number] = jnp.where(first_side, turned[half:], turned[:half])


def image_kernel(own_ref, got_ref, table_ref, *refs):
    out_refs, (power_ref, weight_ref, image_ref) = refs[:-3], refs[-3:]
    blocks = own_ref.shape[1]
    part_width = own_ref.shape[2]
    width = 2 * part_width
    for part, ref in enumerate((own_ref, got_ref)):
        lanes = slice(part * part_width, (part + 1) * part_width)
        weight_ref[0, :, lanes] = ref[0]
        weight_ref[1, :, lanes] = ref[1]
        for coord in range(2):
            angle = ref[2 + coord] * (full_turn / SUB)
            power = (jnp.cos(angle), jnp.sin(angle))
            for step in range(5):
                power_ref[coord, step, 0, :, lanes] = power[0]
                power_ref[coord, step, 1, :, lanes] = power[1]
                power = cmul(power, power)

    sublane = lax.broadcasted_iota(jnp.int32, (8, width), 0)
    marks = [(sublane & (1 << bit)) != 0 for bit in range(3)]
    lane = lax.broadcasted_iota(jnp.int32, (2 * SUB, 128), 1)

    def phasors(coord, block, weight):
        def row(step):
            return (
                power_ref[coord, step, 0, pl.ds(block, 1), :],
                power_ref[coord, step, 1, pl.ds(block, 1), :],
            )

        base = weight
        for bit in range(3):
            step = row(bit)
            factor = (jnp.where(marks[bit], step[0], 1.0), jnp.where(marks[bit], step[1], 0.0))
            base = factor if base is None else cmul(base, factor)
        eighth, sixteenth = row(3), row(4)
        groups = [
            cmul(base, (sixteenth[0], -sixteenth[1])),
            cmul(base, (eighth[0], -eighth[1])),
            base,
            cmul(base, eighth),
        ]
        both = jnp.concatenate([g[0] for g in groups] + [g[1] for g in groups], axis=0)
        high, low = split_value(both)
        return jnp.concatenate([high, low], axis=0)

    def one_block(block):
        weight = (weight_ref[0, pl.ds(block, 1), :], weight_ref[1, pl.ds(block, 1), :])
        first = phasors(0, block, weight)
        second = phasors(1, block, None)
        product = lax.dot_general(
            second, first, (((1,), (1,)), ((), ())), preferred_element_type=f32
        )
        product = product[: 2 * SUB] + product[2 * SUB :]
        return product + pltpu.roll(product, 64, 1)

    def one_pair(pair, carry):
        images = jnp.where(lane < 64, one_block(2 * pair), one_block(2 * pair + 1))
        image_ref[:, pl.ds(pl.multiple_of(pair * 128, 128), 128)] = images
        return carry

    lax.fori_loop(0, blocks // 2, one_pair, 0, unroll=4)

    span = 1024
    for start in range(0, blocks * 64, span):
        high, low = split_value(image_ref[:, start : start + span])
        turned = jnp.dot(
            table_ref[...],
            jnp.concatenate([high, low, high, low], axis=0),
            preferred_element_type=f32,
        )
        for out_ref, (first, last) in zip(out_refs, chunk_rows()):
            count = last - first
            real_lane = lax.broadcasted_iota(jnp.int32, (count, span), 1) % 64 < 32
            upper = turned[2 * first : 2 * first + count]
            lower = turned[2 * first + count : 2 * last]
            swapped = jnp.where(
                real_lane, -pltpu.roll(lower, span - 32, 1), pltpu.roll(lower, 32, 1)
            )
            tiles = upper + swapped
            for pair in range(span // 128):
                out_ref[start // 128 + pair] = tiles[:, pair * 128 : (pair + 1) * 128]


def add(left, right):
    return left[0] + right[0], left[1] + right[1]


def sub(left, right):
    return left[0] - right[0], left[1] - right[1]


def quarter(value):
    return -value[1], value[0]


def fourier_four(x):
    even_sum, even_diff = add(x[0], x[2]), sub(x[0], x[2])
    odd_sum, odd_diff = add(x[1], x[3]), quarter(sub(x[1], x[3]))
    return [
        add(even_sum, odd_sum),
        add(even_diff, odd_diff),
        sub(even_sum, odd_sum),
        sub(even_diff, odd_diff),
    ]


def fourier_eight(x):
    even, odd = fourier_four(x[0::2]), fourier_four(x[1::2])
    half = math.sqrt(0.5)
    odd = [
        odd[0],
        ((odd[1][0] - odd[1][1]) * half, (odd[1][0] + odd[1][1]) * half),
        quarter(odd[2]),
        ((-odd[3][0] - odd[3][1]) * half, (odd[3][0] - odd[3][1]) * half),
    ]
    return [add(even[k], odd[k]) for k in range(4)] + [sub(even[k], odd[k]) for k in range(4)]


def accumulate_kernel(
    source_count, carried, tile_row_ref, tile_column_ref, base_ref, band_ref, *refs
):
    table_ref, twin_table_ref, phase_ref = refs[source_count : source_count + 3]
    out_ref, twin_out_ref, tile_ref, phases_ref, semaphores = refs[-5:]
    slots, group, cells = tile_ref.shape[:3]
    part = slots // source_count
    copies = [
        pltpu.make_async_copy(
            source, tile_ref.at[pl.ds(number * part, part)], semaphores.at[number]
        )
        for number, source in enumerate(refs[:source_count])
    ]
    for copy in copies:
        copy.start()

    for number, ref in enumerate((out_ref, twin_out_ref)):
        if carried:
            ref[...] = refs[source_count + 3 + number][...]
        else:
            ref[...] = jnp.zeros(ref.shape, f32)

    def widen(row, carry):
        phases_ref[row] = jnp.broadcast_to(phase_ref[pl.ds(row, 1), :], phases_ref.shape[1:])
        return carry

    lax.fori_loop(0, phases_ref.shape[0], widen, 0, unroll=8)

    lane = lax.broadcasted_iota(jnp.int32, (group * cells, 128), 1)

    def rowed_tiles(slot):
        values = tile_ref[slot].reshape(group * cells, 128)
        high = values.astype(bf16).astype(f32)
        low = values - high
        evens = jnp.where(lane < 64, high, pltpu.roll(low, 64, 1)).astype(bf16)
        odds = jnp.where(lane < 64, pltpu.roll(high, 64, 1), low).astype(bf16)
        operand = jnp.concatenate([evens, odds], axis=0)
        operand = jnp.concatenate([operand, operand], axis=1)
        return [
            jnp.dot(operand, ref[...], preferred_element_type=f32)
            for ref in (table_ref, twin_table_ref)
        ]

    def spread(rowed, slot):
        base, band = base_ref[slot], band_ref[slot]
        for pair in range(group):
            for side in range(2):
                tile = base + 2 * pair + side
                row, column = tile_row_ref[tile], band + tile_column_ref[tile]
                start = (side * group + pair) * cells
                phase = phases_ref[row, :, :ROWS], phases_ref[row, :, ROWS:]
                for number, acc_ref in enumerate((out_ref, twin_out_ref)):
                    value = rowed[number][start : start + cells]
                    value = cmul((value[:, :ROWS], value[:, ROWS:]), phase)
                    acc_ref[column, :, :ROWS] += value[0]
                    acc_ref[column, :, ROWS:] += value[1]

    def two_slots(turn, carry):
        for number, copy in enumerate(copies):

            @pl.when(turn == number * part // 2)
            def _():
                copy.wait()

        rowed = [rowed_tiles(2 * turn + number) for number in range(2)]
        for number in range(2):
            spread(rowed[number], 2 * turn + number)
        return carry

    lax.fori_loop(0, slots // 2, two_slots, 0)


def transform_kernel(acc_ref, got_ref, column_ref, coarse_ref, fine_ref, out_ref, turned_ref):
    cells = acc_ref.shape[1]
    for cell in range(cells):
        value = acc_ref[:, cell, :] + got_ref[:, cell, :]
        turned = jnp.concatenate(
            [value[:, :ROWS].T, value[:, ROWS:].T], axis=1
        )
        high, low = split_value(turned)
        turned_ref[cell] = (
            jnp.dot(high, column_ref[0], preferred_element_type=f32)
            + jnp.dot(low, column_ref[0], preferred_element_type=f32)
            + jnp.dot(high, column_ref[1], preferred_element_type=f32)
        )
    for fine in range(cells // 4):

        def some_rows(turn, carry):
            rows = pl.ds(pl.multiple_of(turn * 8, 8), 8)
            parts = []
            for coarse in range(4):
                value = (
                    turned_ref[4 * fine + coarse, rows, :256],
                    turned_ref[4 * fine + coarse, rows, 256:],
                )
                if coarse:
                    value = cmul(
                        value,
                        (coarse_ref[coarse, 0:1, :], coarse_ref[coarse, 1:2, :]),
                    )
                parts.append(value)
            for k, value in enumerate(fourier_four(parts)):
                value = cmul(value, (fine_ref[fine, k, 0:1, :], fine_ref[fine, k, 1:2, :]))
                out_ref[fine, k, rows, :256] = value[0]
                out_ref[fine, k, rows, 256:] = value[1]
            return carry

        lax.fori_loop(0, ROWS // 8, some_rows, 0, unroll=2)


def cells_kernel(*refs):
    chunk_refs, out_ref = refs[:-1], refs[-1]
    group_rows = out_ref.shape[1]
    for start_row in range(0, group_rows, 8):
        rows = slice(start_row, start_row + 8)
        for start_lane in range(0, 256, 128):
            re_lanes = slice(start_lane, start_lane + 128)
            im_lanes = slice(256 + start_lane, 256 + start_lane + 128)
            for k in range(4):
                parts = [
                    (ref[fine, k, rows, re_lanes], ref[fine, k, rows, im_lanes])
                    for ref in chunk_refs
                    for fine in range(ref.shape[0])
                ]
                for high_k, value in enumerate(fourier_eight(parts)):
                    start = (k + 4 * high_k) * 256 + start_lane
                    out_ref[0, rows, start : start + 128] = value[0]
                    out_ref[1, rows, start : start + 128] = value[1]


def whole(shape):
    return pl.BlockSpec(shape, lambda *_: (0,) * len(shape))


def params(mib):
    return pltpu.CompilerParams(vmem_limit_bytes=mib * MIB)


Z_SIZE = 4


def bt_moves(bt_count):
    inner = bt_count // Z_SIZE
    places = range(bt_count)
    z_swaps = [[(b, b ^ (k * inner)) for b in places] for k in range(1, Z_SIZE)]
    return z_swaps, [(b, b ^ 2) for b in places], [(b, b ^ 1) for b in places]


def slot_tables(bt_position, ch_position, bt_count, per_band):
    inner = bt_count // Z_SIZE
    z_position, rest = bt_position // inner, bt_position % inner

    def base(k, x, y, half):
        origin = (z_position ^ k) * inner + (rest ^ (2 * x))
        return (origin * 2 + (ch_position ^ y)) * per_band + half * 2 * SLOT

    sides = [(x, y) for x, y in ((0, 0), (1, 0), (0, 1)) for _ in range(2 * Z_SIZE)]
    bases = [base(k // 2 % Z_SIZE, x, y, k % 2) for k, (x, y) in enumerate(sides)]
    ends = [base(k, 1, 1, half) for half in range(2) for k in range(Z_SIZE)]
    band = per_band
    return (
        (jnp.stack(bases).astype(jnp.int32), jnp.asarray([band * y for _, y in sides], jnp.int32)),
        (jnp.stack(ends).astype(jnp.int32), jnp.full((2 * Z_SIZE,), band, jnp.int32)),
    )


def gather_and_work(chunks, bt_count, accumulate, transform):
    z_swaps, x_swap, core_swap = bt_moves(bt_count)
    y_swap = [(0, 1), (1, 0)]
    count = len(chunks)

    def swap(value, pairs):
        return lax.ppermute(value, "bt", pairs)

    def after(value, *others):
        return lax.optimization_barrier((value, *others))[0]

    def next_to(value):
        return jnp.stack([value, swap(value, z_swaps[0])])

    def across(own):
        return [swap(own, x_swap), lax.ppermute(own, "ch", y_swap)]

    def corners(across_x, across_y):
        return [
            lax.ppermute(across_x[:, :SLOT], "ch", y_swap),
            swap(across_y[:, SLOT:], x_swap),
        ]

    def tied(*values):
        return lax.optimization_barrier(values)

    turned = []
    waiting = None
    own = jnp.stack([chunks[0]] + [swap(chunks[0], pairs) for pairs in z_swaps])
    couple = next_to(chunks[1])
    own, couple = tied(own, couple)
    other_couple = swap(couple, z_swaps[1])
    next_couple = next_to(after(chunks[2], own))
    sides = across(own)
    sides, other_couple, next_couple = tied(sides, other_couple, next_couple)
    for chunk in range(count):
        following = chunk + 1 < count
        ends = corners(*sides)
        if following:
            next_own = jnp.concatenate([couple, other_couple], axis=0)
            next_sides = across(next_own)
        other_couple = swap(next_couple, z_swaps[1]) if chunk + 2 < count else ()
        acc = accumulate([own, *sides], None)
        ends, acc, other_couple, waiting = tied(ends, acc, other_couple, waiting)
        couple, next_couple = next_couple, ()
        if chunk + 3 < count:
            next_couple = next_to(after(chunks[chunk + 3], *ends))
        if waiting is not None:
            got = swap(waiting[1], core_swap)
        kept, sent = accumulate(ends, acc)
        if waiting is not None:
            got, kept, sent = tied(got, kept, sent)
            kept, value = tied(kept, transform(chunk - 1, waiting[0], got))
            turned.append(value)
        if following:
            next_sides, kept, sent, next_couple = tied(next_sides, kept, sent, next_couple)
            own, sides = next_own, next_sides
        waiting = (kept, sent)
    turned.append(transform(count - 1, kept, swap(sent, core_swap)))
    return turned


def gathered_shards(visibility, cell_offset, station_gain, stations, row_band, tile_offset):
    bt_count = lax.axis_size("bt")
    ch_count = lax.axis_size("ch")
    ch_position = lax.axis_index("ch")
    device = lax.axis_index("bt") * ch_count + ch_position
    blocks = visibility.shape[3]
    per_band = blocks // ch_count
    tiles_across = G1 * G2 // SUB
    rows_band = tiles_across // bt_count
    cols_band = tiles_across // ch_count
    vis_count = TSLOT * visibility.shape[2]
    pairs = per_band // 2

    part = jax.ShapeDtypeStruct((4, per_band, vis_count), f32)
    own, other = pl.pallas_call(
        weigh_kernel,
        in_specs=[pl.BlockSpec(memory_space=pltpu.SMEM)]
        + [pl.BlockSpec(memory_space=pltpu.VMEM)] * 4,
        out_shape=(part, part),
        compiler_params=params(16),
        name="weigh",
    )(
        ch_position.reshape(1),
        visibility,
        cell_offset,
        station_gain.reshape(-1, station_gain.shape[2]),
        stations.T,
    )
    got = lax.ppermute(other, "ch", [(0, 1), (1, 0)])
    chunks = pl.pallas_call(
        image_kernel,
        out_shape=[
            jax.ShapeDtypeStruct((pairs, last - first, 128), f32) for first, last in chunk_rows()
        ],
        scratch_shapes=[
            pltpu.VMEM((2, 5, 2, per_band, 2 * vis_count), f32),
            pltpu.VMEM((2, per_band, 2 * vis_count), f32),
            pltpu.VMEM((2 * SUB, per_band * 64), f32),
        ],
        compiler_params=params(24),
        name="image",
    )(own, got, jnp.asarray(subgrid_side_table()))

    tile_row = row_band[:, 0] * rows_band + tile_offset // cols_band
    tile_column = tile_offset % cols_band
    all_tables = jnp.asarray(row_tables(bt_count * ch_count))
    table, twin_table = [
        lax.dynamic_index_in_dim(all_tables, number, 0, keepdims=False)
        for number in (device, device ^ ch_count)
    ]
    column_tables = np.stack([tile_column_tables(c * cols_band) for c in range(ch_count)])
    bt_position = lax.axis_index("bt")
    column_table = lax.dynamic_index_in_dim(
        jnp.asarray(column_tables), ch_position, 0, keepdims=False
    )
    tables = slot_tables(bt_position, ch_position, bt_count, per_band)
    acc_shape = jax.ShapeDtypeStruct((tiles_across, CELLS, 2 * ROWS), f32)
    middle = jax.ShapeDtypeStruct((CELLS // 4, 4, ROWS, 512), f32)

    def accumulate(arrays, acc):
        bases, bands = tables[1 if acc else 0]
        slots = bases.shape[0]
        arrays = [array.reshape(-1, SLOT, CELLS, 128) for array in arrays]
        carried = list(acc or ())
        first = 4 + len(arrays) + 3
        return pl.pallas_call(
            functools.partial(accumulate_kernel, len(arrays), bool(acc)),
            in_specs=[pl.BlockSpec(memory_space=pltpu.SMEM)] * 4
            + [pl.BlockSpec(memory_space=pltpu.HBM)] * len(arrays)
            + [pl.BlockSpec(memory_space=pltpu.VMEM)] * (3 + len(carried)),
            scratch_shapes=[
                pltpu.VMEM((slots, SLOT, CELLS, 128), f32),
                pltpu.VMEM((256, CELLS, 2 * ROWS), f32),
                pltpu.SemaphoreType.DMA((len(arrays),)),
            ],
            out_shape=(acc_shape, acc_shape),
            input_output_aliases={first + number: number for number in range(len(carried))},
            compiler_params=params(24),
            cost_estimate=pl.CostEstimate(
                flops=slots * 10**9 * 3 // 4, bytes_accessed=slots * MIB // 2, transcendentals=0
            ),
            name="accumulate",
        )(
            tile_row,
            tile_column,
            bases,
            bands,
            *arrays,
            table,
            twin_table,
            jnp.asarray(tile_row_phases()),
            *carried,
        )

    def transform(chunk, kept, got):
        first = chunk * CELLS // 4
        return pl.pallas_call(
            transform_kernel,
            scratch_shapes=[pltpu.VMEM((CELLS, ROWS, 512), f32)],
            out_shape=middle,
            compiler_params=params(12),
            cost_estimate=pl.CostEstimate(
                flops=8 * 10**9, bytes_accessed=8 * MIB, transcendentals=0
            ),
            name="transform",
        )(
            kept,
            got,
            column_table,
            jnp.asarray(coarse_twiddles()),
            jnp.asarray(fine_twiddles()[first : first + CELLS // 4]),
        )

    turned = gather_and_work(chunks, bt_count, accumulate, transform)
    row_step = 32
    return pl.pallas_call(
        cells_kernel,
        grid=(ROWS // row_step,),
        in_specs=[pl.BlockSpec((CELLS // 4, 4, row_step, 512), lambda i: (0, 0, i, 0))]
        * len(turned),
        out_specs=pl.BlockSpec((2, row_step, G1 * G2), lambda i: (0, i, 0)),
        out_shape=jax.ShapeDtypeStruct((2, ROWS, G1 * G2), f32),
        compiler_params=params(28),
        name="cells",
    )(*turned)


def solution(mesh):
    rows = G1 * G2 // mesh.size
    body = gathered_shards if rows == ROWS and mesh.shape["ch"] == 2 else shards
    return jax.shard_map(
        body,
        mesh=mesh,
        in_specs=(
            P(None, None, "ch", "bt"),
            P(None, None, "ch", "bt"),
            P(None, "ch", None),
            P("bt", None),
            P(),
            P(),
        ),
        out_specs=P(None, ("bt", "ch"), None),
        check_vma=False,
    )
```

```python
import functools
import math

import jax
import jax.numpy as jnp
import numpy as np
from jax import lax
from jax.experimental import pallas as pl
from jax.experimental.pallas import tpu as pltpu
from jax.sharding import PartitionSpec as P

SUB = 32
G1 = 64
G2 = 128
TSLOT = 4
CHANNELS = 64


highest = lax.Precision.HIGHEST
full_turn = 2.0 * math.pi


def complex_einsum(form, left_side, right_side):
    real_part = jnp.einsum(form, left_side[0], right_side[0], precision=highest) - jnp.einsum(
        form, left_side[1], right_side[1], precision=highest
    )
    imag_part = jnp.einsum(form, left_side[0], right_side[1], precision=highest) + jnp.einsum(
        form, left_side[1], right_side[0], precision=highest
    )
    return jnp.stack([real_part, imag_part])


def complex_product(left_side, right_side):
    return jnp.stack(
        [
            left_side[0] * right_side[0] - left_side[1] * right_side[1],
            left_side[0] * right_side[1] + left_side[1] * right_side[0],
        ]
    )


def centred_offsets(length):
    return (jnp.arange(length, dtype=jnp.float32) - length // 2) / length


def phasor_pair(coords, length):
    angles = (full_turn * centred_offsets(length))[None, :, None] * coords[:, None, :]
    return jnp.stack([jnp.cos(angles), jnp.sin(angles)])


def tile_table(length):
    positions = jnp.arange(length, dtype=jnp.int32)
    product = positions[:, None] * (positions[None, :] - length // 2) % length
    angles = -full_turn * product.astype(jnp.float32) / length
    centred = centred_offsets(length)
    tapers = jnp.exp(-4.0 * centred * centred) / math.sqrt(length)
    return jnp.stack([jnp.cos(angles) * tapers[None, :], jnp.sin(angles) * tapers[None, :]])


def weighted_vis(visibility, gain_first, gain_second):
    product_real = gain_first[0] * gain_second[0] + gain_first[1] * gain_second[1]
    product_imag = gain_first[1] * gain_second[0] - gain_first[0] * gain_second[1]
    real_part = visibility[0] * product_real[None] - visibility[1] * product_imag[None]
    imag_part = visibility[0] * product_imag[None] + visibility[1] * product_real[None]
    return jnp.stack([real_part, imag_part])


def image_subgrids(weighted, coords):
    phase_first = phasor_pair(coords[0], SUB)
    phase_second = phasor_pair(coords[1], SUB)
    scaled = jnp.stack(
        [
            weighted[0][:, None, :] * phase_first[0] - weighted[1][:, None, :] * phase_first[1],
            weighted[0][:, None, :] * phase_first[1] + weighted[1][:, None, :] * phase_first[0],
        ]
    )
    return complex_einsum("klb,kmb->lmb", scaled, phase_second)


def to_tiles(subgrid_image):
    factor_table = tile_table(SUB)
    partial_value = complex_einsum("pl,lmb->pmb", factor_table, subgrid_image)
    return complex_einsum("qm,pmb->pqb", factor_table, partial_value)


def dft_table(length):
    positions = jnp.arange(length, dtype=jnp.int32)
    angles = (
        full_turn * (positions[:, None] * positions[None, :] % length).astype(jnp.float32) / length
    )
    return jnp.stack([jnp.cos(angles), jnp.sin(angles)])


def twiddle_table(outer_length, inner_length):
    full_length = outer_length * inner_length
    outer_index = jnp.arange(outer_length, dtype=jnp.int32)
    inner_index = jnp.arange(inner_length, dtype=jnp.int32)
    angles = (
        full_turn
        * (outer_index[:, None] * inner_index[None, :] % full_length).astype(jnp.float32)
        / full_length
    )
    return jnp.stack([jnp.cos(angles), jnp.sin(angles)])


def transform_rows(cells):
    columns = cells.shape[2]
    blocked = cells.reshape(2, G1, G2, columns)
    section_one = complex_einsum("kn,nmc->kmc", dft_table(G1), blocked)
    section_one = complex_product(section_one, twiddle_table(G1, G2)[:, :, :, None])
    section_two = complex_einsum("mn,knc->mkc", dft_table(G2), section_one)
    return section_two.reshape(2, G1 * G2, columns)


def transform_columns(cells):
    row_count = cells.shape[1]
    blocked = cells.reshape(2, row_count, G1, G2)
    section_one = complex_einsum("kn,rnm->rkm", dft_table(G1), blocked)
    section_one = complex_product(section_one, twiddle_table(G1, G2)[:, None, :, :])
    section_two = complex_einsum("mn,rkn->rmk", dft_table(G2), section_one)
    return section_two.reshape(2, row_count, G1 * G2)


def band_ranks(bands, band_count):
    marked = (bands[:, :, None] == jnp.arange(band_count, dtype=jnp.int32)[None, None, :]).astype(
        jnp.int32
    )
    before = jnp.cumsum(marked, axis=1) - marked
    return jnp.sum(before * marked, axis=2)


def station_pick(chosen, station_count):
    return (jnp.arange(station_count, dtype=jnp.int32)[:, None] == chosen[None, :]).astype(
        jnp.float32
    )


def shards(visibility, cell_offset, station_gain, stations, row_band, tile_offset):
    bt_count = lax.axis_size("bt")
    ch_count = lax.axis_size("ch")
    bt_position = lax.axis_index("bt")
    ch_position = lax.axis_index("ch")
    blocks = visibility.shape[3]
    per_band = blocks // ch_count
    tiles_across = G1 * G2 // SUB
    rows_band = tiles_across // bt_count
    cols_band = tiles_across // ch_count
    capacity = max(2, 2 * blocks // (ch_count * bt_count))
    slot_count = bt_count * capacity
    station_count = station_gain.shape[2]
    gain_first = jnp.einsum(
        "xcs,sb->xcb", station_gain, station_pick(stations[:, 0], station_count), precision=highest
    )
    gain_second = jnp.einsum(
        "xcs,sb->xcb", station_gain, station_pick(stations[:, 1], station_count), precision=highest
    )
    weighted_full = weighted_vis(visibility, gain_first, gain_second)
    band_weights, band_coords = (
        lax.all_to_all(weighted_full, "ch", split_axis=3, concat_axis=2, tiled=True),
        lax.all_to_all(cell_offset, "ch", split_axis=3, concat_axis=2, tiled=True),
    )
    tile_stack = to_tiles(
        image_subgrids(band_weights.reshape(2, -1, per_band), band_coords.reshape(2, -1, per_band))
    )
    band_table = row_band.reshape(bt_count, blocks)
    band_part = lax.dynamic_slice_in_dim(band_table, ch_position * per_band, per_band, 1)
    rank_part = band_ranks(band_part, bt_count)
    own_band = lax.dynamic_index_in_dim(band_part, bt_position, 0, keepdims=False)
    own_rank = lax.dynamic_index_in_dim(rank_part, bt_position, 0, keepdims=False)
    own_slot = own_band * capacity + own_rank
    slot_range = jnp.arange(slot_count, dtype=jnp.int32)
    chooser = (own_slot[:, None] == slot_range[None, :]).astype(jnp.float32)
    outbound = jnp.einsum("xpqw,ws->xpqs", tile_stack, chooser, precision=highest)
    inbound = lax.all_to_all(outbound, "bt", split_axis=3, concat_axis=3, tiled=True)
    landed = band_part == bt_position
    slot_index = jnp.arange(bt_count, dtype=jnp.int32)[:, None] * capacity + rank_part
    slot_hits = ((slot_index[:, :, None] == slot_range[None, None, :]) & landed[:, :, None]).astype(
        jnp.float32
    )
    offset_table = tile_offset.reshape(bt_count, blocks)
    offset_part = lax.dynamic_slice_in_dim(offset_table, ch_position * per_band, per_band, 1)
    tile_range = jnp.arange(rows_band * cols_band, dtype=jnp.int32)
    tile_hits = (offset_part[:, :, None] == tile_range[None, None, :]).astype(jnp.float32)
    placing = jnp.einsum("iws,iwt->st", slot_hits, tile_hits, precision=highest)
    placed = jnp.einsum("xpqs,st->xpqt", inbound, placing, precision=highest)
    grid_block = placed.reshape(2, SUB, SUB, rows_band, cols_band).transpose(0, 3, 1, 4, 2)
    grid_block = grid_block.reshape(2, rows_band * SUB, cols_band * SUB)
    row_span = grid_block.shape[1]
    narrow = grid_block.shape[2] // bt_count
    sending = (
        grid_block.reshape(2, row_span, bt_count, narrow)
        .transpose(0, 2, 1, 3)
        .reshape(2, bt_count, row_span * narrow)
    )
    gathered = lax.all_to_all(sending, "bt", split_axis=1, concat_axis=1, tiled=True)
    along_rows = transform_rows(gathered.reshape(2, bt_count * row_span, narrow))
    spread = lax.all_to_all(
        lax.all_to_all(along_rows, "bt", split_axis=1, concat_axis=2, tiled=True),
        "ch",
        split_axis=1,
        concat_axis=2,
        tiled=True,
    )
    scale = 1.0 / (G1 * G2 * math.sqrt(TSLOT * CHANNELS))
    return transform_columns(spread) * scale

ROWS = 256
CHUNKS = 4
CELLS = 8
SLOT = 32
MIB = 1024 * 1024
f32 = jnp.float32
bf16 = jnp.bfloat16


def split_table(table):
    table = np.asarray(table, np.float64)
    high = table.astype(np.float32).astype(bf16)
    low = (table - high.astype(np.float64)).astype(np.float32).astype(bf16)
    return high, low


def real_form(table):
    return np.block([[table.real, table.imag], [-table.imag, table.real]])


def tile_matrix():
    index = np.arange(SUB)
    centred = (index - SUB // 2) / SUB
    taper = np.exp(-4.0 * centred * centred) / math.sqrt(SUB)
    return np.exp(-2j * math.pi * index[:, None] * centred[None, :]) * taper[None, :]


def cell_order():
    return [8 * coarse + fine for fine in range(8) for coarse in range(4)]


def chunk_rows():
    return [(chunk * CELLS, (chunk + 1) * CELLS) for chunk in range(CHUNKS)]


def subgrid_side_table():
    ordered = tile_matrix()[cell_order()]
    sides = real_form(ordered.T).T.reshape(2, SUB, 2 * SUB)
    rows = [sides[:, start:end].reshape(-1, 2 * SUB) for start, end in chunk_rows()]
    high, low = split_table(np.concatenate(rows, axis=0))
    return np.concatenate([high, high, low, low], axis=1)


def row_tables(devices):
    length = G1 * G2
    rows = np.arange(length)
    turn = (rows[:, None] * np.arange(SUB)[None, :]) % length
    full = np.exp(2j * math.pi * turn / length) @ tile_matrix()
    tables = []
    for device in range(devices):
        part = full[device * ROWS : (device + 1) * ROWS].T
        high, low = split_table(real_form(part))
        tables.append(np.concatenate([high, high, low, low], axis=0))
    return np.stack(tables)


def tile_row_phases():
    angle = 2 * math.pi * (np.outer(np.arange(256), np.arange(ROWS)) % 256) / 256
    table = np.concatenate([np.cos(angle), np.sin(angle)], axis=1).astype(np.float32)
    return np.ascontiguousarray(np.broadcast_to(table[:, None, :], (256, CELLS, 2 * ROWS)))


def tile_column_tables(first_column):
    scale = 1.0 / (G1 * G2 * math.sqrt(TSLOT * CHANNELS))
    index = np.arange(256)
    turn = np.outer((index + first_column) % 256, index) % 256
    high, low = split_table(real_form(np.exp(2j * math.pi * turn / 256) * scale))
    return np.stack([high, low])


def coarse_twiddles():
    angle = 2 * math.pi * np.outer(np.arange(4), np.arange(256)) / 1024
    return np.stack([np.cos(angle), np.sin(angle)], axis=1).astype(np.float32)


def fine_twiddles():
    turn = np.arange(4)[:, None] * 256 + np.arange(256)[None, :]
    angle = 2 * math.pi * np.arange(8)[:, None, None] * turn[None] / (G1 * G2)
    return np.stack([np.cos(angle), np.sin(angle)], axis=2).astype(np.float32)


def split_value(value):
    high = value.astype(bf16)
    low = (value - high.astype(f32)).astype(bf16)
    return high, low


def cmul(left, right):
    return (
        left[0] * right[0] - left[1] * right[1],
        left[0] * right[1] + left[1] * right[0],
    )


def weigh_kernel(position_ref, vis_ref, off_ref, gain_ref, station_ref, own_ref, other_ref):
    station_count = gain_ref.shape[1]
    blocks = station_ref.shape[1]
    channels = vis_ref.shape[2]
    numbers = lax.broadcasted_iota(jnp.int32, (station_count, blocks), 0)
    gains = gain_ref[...]

    def pick(which):
        chosen = (numbers == station_ref[which : which + 1, :]).astype(f32)
        return jnp.dot(gains, chosen, precision=highest, preferred_element_type=f32)

    first, second = pick(0), pick(1)
    first_re, first_im = first[:channels], first[channels:]
    second_re, second_im = second[:channels], second[channels:]
    gain = (
        first_re * second_re + first_im * second_im,
        first_im * second_re - first_re * second_im,
    )
    weighted = [cmul((vis_ref[0, t], vis_ref[1, t]), gain) for t in range(TSLOT)]
    planes = [
        jnp.concatenate([w[0] for w in weighted], axis=0),
        jnp.concatenate([w[1] for w in weighted], axis=0),
        jnp.concatenate([off_ref[0, t] for t in range(TSLOT)], axis=0),
        jnp.concatenate([off_ref[1, t] for t in range(TSLOT)], axis=0),
    ]
    half = blocks // 2
    first_side = position_ref[0] == 0
    for number, plane in enumerate(planes):
        turned = plane.T
        own_ref[number] = jnp.where(first_side, turned[:half], turned[half:])
        other_ref[number] = jnp.where(first_side, turned[half:], turned[:half])


def image_kernel(own_ref, got_ref, table_ref, *refs):
    out_refs, (power_ref, weight_ref, image_ref) = refs[:-3], refs[-3:]
    blocks = own_ref.shape[1]
    part_width = own_ref.shape[2]
    width = 2 * part_width
    for part, ref in enumerate((own_ref, got_ref)):
        lanes = slice(part * part_width, (part + 1) * part_width)
        weight_ref[0, :, lanes] = ref[0]
        weight_ref[1, :, lanes] = ref[1]
        for coord in range(2):
            angle = ref[2 + coord] * (full_turn / SUB)
            power = (jnp.cos(angle), jnp.sin(angle))
            for step in range(5):
                power_ref[coord, step, 0, :, lanes] = power[0]
                power_ref[coord, step, 1, :, lanes] = power[1]
                power = cmul(power, power)

    sublane = lax.broadcasted_iota(jnp.int32, (8, width), 0)
    marks = [(sublane & (1 << bit)) != 0 for bit in range(3)]
    lane = lax.broadcasted_iota(jnp.int32, (2 * SUB, 128), 1)

    def phasors(coord, block, weight):
        def row(step):
            return (
                power_ref[coord, step, 0, pl.ds(block, 1), :],
                power_ref[coord, step, 1, pl.ds(block, 1), :],
            )

        base = weight
        for bit in range(3):
            step = row(bit)
            factor = (jnp.where(marks[bit], step[0], 1.0), jnp.where(marks[bit], step[1], 0.0))
            base = factor if base is None else cmul(base, factor)
        eighth, sixteenth = row(3), row(4)
        groups = [
            cmul(base, (sixteenth[0], -sixteenth[1])),
            cmul(base, (eighth[0], -eighth[1])),
            base,
            cmul(base, eighth),
        ]
        both = jnp.concatenate([g[0] for g in groups] + [g[1] for g in groups], axis=0)
        high, low = split_value(both)
        return jnp.concatenate([high, low], axis=0)

    def one_block(block):
        weight = (weight_ref[0, pl.ds(block, 1), :], weight_ref[1, pl.ds(block, 1), :])
        first = phasors(0, block, weight)
        second = phasors(1, block, None)
        product = lax.dot_general(
            second, first, (((1,), (1,)), ((), ())), preferred_element_type=f32
        )
        product = product[: 2 * SUB] + product[2 * SUB :]
        return product + pltpu.roll(product, 64, 1)

    def one_pair(pair, carry):
        images = jnp.where(lane < 64, one_block(2 * pair), one_block(2 * pair + 1))
        image_ref[:, pl.ds(pl.multiple_of(pair * 128, 128), 128)] = images
        return carry

    lax.fori_loop(0, blocks // 2, one_pair, 0, unroll=4)

    span = 1024
    for start in range(0, blocks * 64, span):
        high, low = split_value(image_ref[:, start : start + span])
        turned = jnp.dot(
            table_ref[...],
            jnp.concatenate([high, low, high, low], axis=0),
            preferred_element_type=f32,
        )
        for out_ref, (first, last) in zip(out_refs, chunk_rows()):
            count = last - first
            real_lane = lax.broadcasted_iota(jnp.int32, (count, span), 1) % 64 < 32
            upper = turned[2 * first : 2 * first + count]
            lower = turned[2 * first + count : 2 * last]
            swapped = jnp.where(
                real_lane, -pltpu.roll(lower, span - 32, 1), pltpu.roll(lower, 32, 1)
            )
            tiles = upper + swapped
            for pair in range(span // 128):
                out_ref[start // 128 + pair] = tiles[:, pair * 128 : (pair + 1) * 128]


def add(left, right):
    return left[0] + right[0], left[1] + right[1]


def sub(left, right):
    return left[0] - right[0], left[1] - right[1]


def quarter(value):
    return -value[1], value[0]


def fourier_four(x):
    even_sum, even_diff = add(x[0], x[2]), sub(x[0], x[2])
    odd_sum, odd_diff = add(x[1], x[3]), quarter(sub(x[1], x[3]))
    return [
        add(even_sum, odd_sum),
        add(even_diff, odd_diff),
        sub(even_sum, odd_sum),
        sub(even_diff, odd_diff),
    ]


def fourier_eight(x):
    even, odd = fourier_four(x[0::2]), fourier_four(x[1::2])
    half = math.sqrt(0.5)
    odd = [
        odd[0],
        ((odd[1][0] - odd[1][1]) * half, (odd[1][0] + odd[1][1]) * half),
        quarter(odd[2]),
        ((-odd[3][0] - odd[3][1]) * half, (odd[3][0] - odd[3][1]) * half),
    ]
    return [add(even[k], odd[k]) for k in range(4)] + [sub(even[k], odd[k]) for k in range(4)]


def tile_sources(refs):
    own, across_x, across_y, corner_first, corner_last = refs
    pieces = []
    for half in range(2):
        pairs = pl.ds(half * SLOT, SLOT)
        corner = (corner_first, corner_last)[half]
        for band, number, source in (
            (0, 0, own.at[:, pairs]),
            (0, 1, across_x.at[:, pairs]),
            (1, 0, across_y.at[:, pairs]),
            (1, 1, corner),
        ):
            pieces.append((source, band, 8 * half + 4 * number))
    return pieces


def accumulate_kernel(tile_row_ref, tile_column_ref, base_ref, *refs):
    (
        table_ref,
        twin_table_ref,
        phases_ref,
        out_ref,
        twin_out_ref,
        tile_ref,
        semaphores,
    ) = refs[-7:]
    slots, cells = tile_ref.shape[1], tile_ref.shape[3]
    group = 16
    slot_groups = SLOT // group
    copies = []
    for number, (source, band, first) in enumerate(tile_sources(refs[:-7])):
        copies.append(
            pltpu.make_async_copy(
                source,
                tile_ref.at[band, pl.ds(first, source.shape[0])],
                semaphores.at[number],
            )
        )
    for copy in copies:
        copy.start()

    for ref in (out_ref, twin_out_ref):
        ref[...] = jnp.zeros(ref.shape, f32)

    for copy in copies[: len(copies) // 2]:
        copy.wait()

    lane = lax.broadcasted_iota(jnp.int32, (group * cells, 128), 1)

    def rowed_tiles(number):
        slot, within = number // slot_groups, number % slot_groups
        start = pl.multiple_of(within * group, group)
        operands = []
        for band in range(2):
            values = tile_ref[band, slot, pl.ds(start, group)].reshape(group * cells, 128)
            high = values.astype(bf16).astype(f32)
            low = values - high
            operands.append(jnp.where(lane < 64, high, pltpu.roll(low, 64, 1)).astype(bf16))
            operands.append(jnp.where(lane < 64, pltpu.roll(high, 64, 1), low).astype(bf16))
        operand = jnp.concatenate(operands, axis=0)
        operand = jnp.concatenate([operand, operand], axis=1)
        return [
            jnp.dot(operand, ref[...], preferred_element_type=f32)
            for ref in (table_ref, twin_table_ref)
        ]

    def spread(rowed, number):
        slot, within = number // slot_groups, number % slot_groups
        bases = [base_ref[band * slots + slot] + within * group * 2 for band in range(2)]
        for pair in range(group):
            for side in range(2):
                for band in range(2):
                    tile = bases[band] + 2 * pair + side
                    row, column = tile_row_ref[tile], tile_column_ref[tile]
                    start = ((2 * band + side) * group + pair) * cells
                    phase = phases_ref[row, :, :ROWS], phases_ref[row, :, ROWS:]
                    for number, acc_ref in enumerate((out_ref, twin_out_ref)):
                        value = rowed[number][start : start + cells]
                        value = cmul((value[:, :ROWS], value[:, ROWS:]), phase)
                        acc_ref[band, column, :, :ROWS] += value[0]
                        acc_ref[band, column, :, ROWS:] += value[1]

    groups = slots * slot_groups

    def two_groups(turn, carry):
        @pl.when(turn == groups // 4)
        def _():
            for copy in copies[len(copies) // 2 :]:
                copy.wait()

        rowed = [rowed_tiles(2 * turn + number) for number in range(2)]
        for number in range(2):
            spread(rowed[number], 2 * turn + number)
        return carry

    lax.fori_loop(0, groups // 2, two_groups, 0)


def transform_kernel(acc_ref, got_ref, column_ref, coarse_ref, fine_ref, out_ref, turned_ref):
    cells = acc_ref.shape[2]
    for cell in range(cells):
        near = acc_ref[0, :, cell, :] + got_ref[0, :, cell, :]
        far = acc_ref[1, :, cell, :] + got_ref[1, :, cell, :]
        turned = jnp.concatenate(
            [near[:, :ROWS].T, far[:, :ROWS].T, near[:, ROWS:].T, far[:, ROWS:].T], axis=1
        )
        high, low = split_value(turned)
        turned_ref[cell] = (
            jnp.dot(high, column_ref[0], preferred_element_type=f32)
            + jnp.dot(low, column_ref[0], preferred_element_type=f32)
            + jnp.dot(high, column_ref[1], preferred_element_type=f32)
        )
    for fine in range(cells // 4):

        def some_rows(turn, carry):
            rows = pl.ds(pl.multiple_of(turn * 8, 8), 8)
            parts = []
            for coarse in range(4):
                value = (
                    turned_ref[4 * fine + coarse, rows, :256],
                    turned_ref[4 * fine + coarse, rows, 256:],
                )
                if coarse:
                    value = cmul(
                        value,
                        (coarse_ref[coarse, 0:1, :], coarse_ref[coarse, 1:2, :]),
                    )
                parts.append(value)
            for k, value in enumerate(fourier_four(parts)):
                value = cmul(value, (fine_ref[fine, k, 0:1, :], fine_ref[fine, k, 1:2, :]))
                out_ref[fine, k, rows, :256] = value[0]
                out_ref[fine, k, rows, 256:] = value[1]
            return carry

        lax.fori_loop(0, ROWS // 8, some_rows, 0, unroll=2)


def cells_kernel(*refs):
    chunk_refs, out_ref = refs[:-1], refs[-1]
    group_rows = out_ref.shape[1]
    for start_row in range(0, group_rows, 8):
        rows = slice(start_row, start_row + 8)
        for start_lane in range(0, 256, 128):
            re_lanes = slice(start_lane, start_lane + 128)
            im_lanes = slice(256 + start_lane, 256 + start_lane + 128)
            for k in range(4):
                parts = [
                    (ref[fine, k, rows, re_lanes], ref[fine, k, rows, im_lanes])
                    for ref in chunk_refs
                    for fine in range(ref.shape[0])
                ]
                for high_k, value in enumerate(fourier_eight(parts)):
                    start = (k + 4 * high_k) * 256 + start_lane
                    out_ref[0, rows, start : start + 128] = value[0]
                    out_ref[1, rows, start : start + 128] = value[1]


def whole(shape):
    return pl.BlockSpec(shape, lambda *_: (0,) * len(shape))


def params(mib):
    return pltpu.CompilerParams(vmem_limit_bytes=mib * MIB)


Z_SIZE = 4


def bt_moves(bt_count):
    inner = bt_count // Z_SIZE
    places = range(bt_count)
    z_swaps = [[(b, b ^ (k * inner)) for b in places] for k in range(1, Z_SIZE)]
    return z_swaps, [(b, b ^ 2) for b in places], [(b, b ^ 1) for b in places]


def tile_bases(bt_position, ch_position, bt_count, per_band):
    inner = bt_count // Z_SIZE
    z_position, rest = bt_position // inner, bt_position % inner
    bases = []
    for ch in (ch_position, 1 - ch_position):
        for half in range(2):
            for x in range(2):
                for k in range(Z_SIZE):
                    origin = (z_position ^ k) * inner + (rest ^ (2 * x))
                    bases.append((origin * 2 + ch) * per_band + half * 2 * SLOT)
    return jnp.stack(bases).astype(jnp.int32)


def gather_and_work(chunks, bt_count, held, accumulate, transform):
    z_swaps, x_swap, core_swap = bt_moves(bt_count)
    y_swap = [(0, 1), (1, 0)]
    count = len(chunks)

    def swap(value, pairs):
        return lax.ppermute(value, "bt", pairs)

    def after(value, *others):
        return lax.optimization_barrier((value, *others))[0]

    def next_to(value):
        return jnp.stack([value, swap(value, z_swaps[0])])

    def across(own):
        return [swap(own, x_swap), lax.ppermute(own, "ch", y_swap)]

    def corners(across_x, across_y):
        return [
            lax.ppermute(across_x[:, :SLOT], "ch", y_swap),
            swap(across_y[:, SLOT:], x_swap),
        ]

    turned = []
    waiting = None
    own = jnp.stack([chunks[0]] + [swap(chunks[0], pairs) for pairs in z_swaps])
    couple = next_to(chunks[1])
    own, couple, ready = lax.optimization_barrier((own, couple, dict(held)))
    held.update(ready)
    other_couple = swap(couple, z_swaps[1])
    second_couple = next_to(after(chunks[2], own))
    sides = across(own)
    for chunk in range(count):
        following = chunk + 1 < count
        if following:
            sides, other_couple, second_couple = lax.optimization_barrier(
                (sides, other_couple, second_couple)
            )
            next_own = jnp.concatenate([couple, other_couple], axis=0)
        ends = corners(*sides)
        if chunk + 2 < count:
            couple = next_to(after(chunks[chunk + 2], *sides)) if chunk else second_couple
            ends, couple = lax.optimization_barrier((ends, couple))
        if chunk > 1:
            ends, value = lax.optimization_barrier((ends, transform(chunk - 2, *waiting)))
            turned.append(value)
        if chunk > 0:
            waiting = (kept, swap(sent, core_swap))
        parts = [own, *sides, *ends]
        if following:
            own, parts[3:] = lax.optimization_barrier((next_own, ends))
            sides = across(own)
        if chunk + 2 < count:
            other_couple = swap(after(couple, own), z_swaps[1])
        kept, sent = accumulate(parts)
        if following:
            sides, other_couple, kept, sent = lax.optimization_barrier(
                (sides, other_couple, kept, sent)
            )
    turned.append(transform(count - 2, *waiting))
    turned.append(transform(count - 1, kept, swap(sent, core_swap)))
    return turned


def gathered_shards(visibility, cell_offset, station_gain, stations, row_band, tile_offset):
    bt_count = lax.axis_size("bt")
    ch_count = lax.axis_size("ch")
    ch_position = lax.axis_index("ch")
    device = lax.axis_index("bt") * ch_count + ch_position
    blocks = visibility.shape[3]
    per_band = blocks // ch_count
    tiles_across = G1 * G2 // SUB
    rows_band = tiles_across // bt_count
    cols_band = tiles_across // ch_count
    vis_count = TSLOT * visibility.shape[2]
    pairs = per_band // 2

    part = jax.ShapeDtypeStruct((4, per_band, vis_count), f32)
    own, other = pl.pallas_call(
        weigh_kernel,
        in_specs=[pl.BlockSpec(memory_space=pltpu.SMEM)]
        + [pl.BlockSpec(memory_space=pltpu.VMEM)] * 4,
        out_shape=(part, part),
        compiler_params=params(16),
        name="weigh",
    )(
        ch_position.reshape(1),
        visibility,
        cell_offset,
        station_gain.reshape(-1, station_gain.shape[2]),
        stations.T,
    )
    got = lax.ppermute(other, "ch", [(0, 1), (1, 0)])
    chunks = pl.pallas_call(
        image_kernel,
        out_shape=[
            jax.ShapeDtypeStruct((pairs, last - first, 128), f32) for first, last in chunk_rows()
        ],
        scratch_shapes=[
            pltpu.VMEM((2, 5, 2, per_band, 2 * vis_count), f32),
            pltpu.VMEM((2, per_band, 2 * vis_count), f32),
            pltpu.VMEM((2 * SUB, per_band * 64), f32),
        ],
        compiler_params=params(24),
        name="image",
    )(own, got, jnp.asarray(subgrid_side_table()))

    tile_row = row_band[:, 0] * rows_band + tile_offset // cols_band
    tile_column = tile_offset % cols_band
    all_tables = jnp.asarray(row_tables(bt_count * ch_count))
    table, twin_table = [
        lax.dynamic_index_in_dim(all_tables, number, 0, keepdims=False)
        for number in (device, device ^ ch_count)
    ]
    column_tables = np.stack([tile_column_tables(c * cols_band) for c in range(ch_count)])
    bt_position = lax.axis_index("bt")
    column_table = lax.dynamic_index_in_dim(
        jnp.asarray(column_tables), ch_position, 0, keepdims=False
    )
    bases = tile_bases(bt_position, ch_position, bt_count, per_band)
    acc = jax.ShapeDtypeStruct((2, cols_band, CELLS, 2 * ROWS), f32)
    middle = jax.ShapeDtypeStruct((CELLS // 4, 4, ROWS, 512), f32)
    slots = bt_count * pairs // (2 * SLOT)

    def accumulate(arrays):
        return pl.pallas_call(
            accumulate_kernel,
            in_specs=[pl.BlockSpec(memory_space=pltpu.SMEM)] * 3
            + [pl.BlockSpec(memory_space=pltpu.HBM)] * len(arrays)
            + [pl.BlockSpec(memory_space=pltpu.VMEM)] * 3,
            scratch_shapes=[
                pltpu.VMEM((2, slots, SLOT, CELLS, 128), f32),
                pltpu.SemaphoreType.DMA((8,)),
            ],
            out_shape=(acc, acc),
            compiler_params=params(14),
            cost_estimate=pl.CostEstimate(
                flops=20 * 10**9, bytes_accessed=16 * MIB, transcendentals=0
            ),
            name="accumulate",
        )(
            *held["places"],
            *arrays,
            *held["tables"],
        )

    def transform(chunk, kept, got):
        first = chunk * CELLS // 4
        return pl.pallas_call(
            transform_kernel,
            scratch_shapes=[pltpu.VMEM((CELLS, ROWS, 512), f32)],
            out_shape=middle,
            compiler_params=params(12),
            cost_estimate=pl.CostEstimate(
                flops=8 * 10**9, bytes_accessed=8 * MIB, transcendentals=0
            ),
            name="transform",
        )(
            kept,
            got,
            held["columns"],
            jnp.asarray(coarse_twiddles()),
            jnp.asarray(fine_twiddles()[first : first + CELLS // 4]),
        )

    held = {
        "places": [tile_row, tile_column, bases],
        "tables": [table, twin_table, jnp.asarray(tile_row_phases())],
        "columns": column_table,
    }
    turned = gather_and_work(chunks, bt_count, held, accumulate, transform)
    row_step = 32
    return pl.pallas_call(
        cells_kernel,
        grid=(ROWS // row_step,),
        in_specs=[pl.BlockSpec((CELLS // 4, 4, row_step, 512), lambda i: (0, 0, i, 0))]
        * len(turned),
        out_specs=pl.BlockSpec((2, row_step, G1 * G2), lambda i: (0, i, 0)),
        out_shape=jax.ShapeDtypeStruct((2, ROWS, G1 * G2), f32),
        compiler_params=params(28),
        name="cells",
    )(*turned)


def solution(mesh):
    rows = G1 * G2 // mesh.size
    body = gathered_shards if rows == ROWS and mesh.shape["ch"] == 2 else shards
    return jax.shard_map(
        body,
        mesh=mesh,
        in_specs=(
            P(None, None, "ch", "bt"),
            P(None, None, "ch", "bt"),
            P(None, "ch", None),
            P("bt", None),
            P(),
            P(),
        ),
        out_specs=P(None, ("bt", "ch"), None),
        check_vma=False,
    )
```
